256 devices in a mesh: sub: 16 (over y, x), grp: 16 (over z, core).
Axes of the slice: x: 4, y: 4, z: 8, core: 2. Of those that a mesh axis runs over, the one named last changes fastest.
Arguments:
- applied_loads: float32 [16, 16, 64, 1536], P('sub', 'grp')
- flex_matrix: bfloat16 [16, 16, 1536, 1536], P('sub', 'grp'), as said below
- schur_matrix: bfloat16 [16, 16, 1536, 1536], P('sub', 'grp'), as said below
- corner_coupling: float32 [16, 16, 12, 1536], P('sub', 'grp'), may hold values from -0.625 to 0.625
- coarse_inverse: float32 [768, 768], replicated, as said below
- face_match: int32 [16, 16, 4, 384], P('sub', 'grp'), may hold values from 0 to 383, as said below
- corner_map: int32 [16, 16, 12], P('sub', 'grp'), may hold values from 0 to 767, as said below
Outputs:
- multipliers: float32 [16, 16, 64, 4, 384], P('sub', 'grp')
- residual: float32 [16, 16, 64, 4, 384], P('sub', 'grp')
The draws below stay inside these ranges and needn't reach their ends.
Inputs may be any that keep to these rules, and one draw needn't show every extreme that they name: `flex_matrix`: each subdomain's matrix is symmetric positive definite. `schur_matrix`: each subdomain's matrix is symmetric positive definite. `coarse_inverse`: lower triangular with a positive diagonal. face_match[s, g, 1] is a permutation of the 384 face nodes and face_match[s+1, g, 0] is its inverse; face_match[s, g, 3] and face_match[s, g+1, 2] likewise (indices wrap). `corner_map`: the 12 entries of one subdomain are distinct; every corner unknown is named by exactly four subdomains.
All inputs are finite; a program needn't handle non-finite values.
Results may differ from the reference program's by a relative error of at most 0.0088.
Values sent between devices are 32-bit elements; how exact they have to be, the bound alone decides.
A program may use at most 64 MiB of HBM per device.

```python
import math
import jax
import jax.numpy as jnp
from jax import lax

FACE = 384
LOADS = 64
DOF_NODE = 3
ITERS = 2
NI = 1536
NCL = 12
NC = 768
N_SUB = 16
N_GRP = 16


def positive_block(key):

    def one_matrix(index):
        subkeys = jax.random.split(jax.random.fold_in(key, index), 2)
        entries = jax.random.normal(subkeys[0], (NI, NI), jnp.float32) * (0.6 / math.sqrt(NI))
        symmetric = (entries + entries.T) * (1.0 / math.sqrt(2.0))
        diagonal = jax.random.uniform(subkeys[1], (NI, 1), jnp.float32, 1.5, 3.0)
        on_diagonal = (jnp.arange(NI)[:, None] == jnp.arange(NI)[None, :]).astype(jnp.float32)
        matrix = symmetric + on_diagonal * diagonal
        return matrix.astype(jnp.bfloat16)
    stacked = lax.map(one_matrix, jnp.arange(N_SUB * N_GRP))
    return stacked.reshape(N_SUB, N_GRP, NI, NI)


def draw_flex_matrix(key, part):
    key = jax.random.fold_in(key, 11)
    return positive_block(key)


def draw_schur_matrix(key, part):
    key = jax.random.fold_in(key, 12)
    return positive_block(key)


def draw_coarse_inverse(key, part):
    key = jax.random.fold_in(key, 13)
    subkeys = jax.random.split(key, 2)
    row_index = jnp.arange(NC)[:, None]
    col_index = jnp.arange(NC)[None, :]
    off_diagonal = jax.random.normal(subkeys[0], (NC, NC), jnp.float32) * (0.3 / math.sqrt(NC))
    diagonal = jax.random.uniform(subkeys[1], (NC, NC), jnp.float32, 0.6, 1.2)
    return jnp.where(row_index > col_index, off_diagonal, 0.0) + jnp.where(row_index == col_index, diagonal, 0.0)


def draw_applied_loads(key, part):
    key = jax.random.fold_in(key, 14)
    subkeys = jax.random.split(key, 1)
    position = (jnp.arange(N_SUB)[:, None] * N_GRP + jnp.arange(N_GRP)[None, :]).astype(jnp.float32)
    factor = 1.0 + 2.0 * position / max(N_SUB * N_GRP - 1, 1)
    entries = jax.random.normal(subkeys[0], (N_SUB, N_GRP, LOADS, NI), jnp.float32)
    return entries * factor[:, :, None, None]


def draw_face_match(key, part):
    key = jax.random.fold_in(key, 15)
    subkeys = jax.random.split(key, 2)

    def orderings(base):
        return jax.vmap(lambda single: jax.random.permutation(single, FACE))(jax.random.split(base, N_SUB * N_GRP)).reshape(N_SUB, N_GRP, FACE).astype(jnp.int32)
    along_sub = orderings(subkeys[0])
    along_grp = orderings(subkeys[1])
    inverse_sub = jnp.argsort(along_sub, axis=-1).astype(jnp.int32)
    inverse_grp = jnp.argsort(along_grp, axis=-1).astype(jnp.int32)
    return jnp.stack([jnp.roll(inverse_sub, 1, axis=0), along_sub, jnp.roll(inverse_grp, 1, axis=1), along_grp], axis=2)


def draw_corner_map(key, part):
    key = jax.random.fold_in(key, 16)
    ordering = jax.random.permutation(key, N_SUB * N_GRP).reshape(N_SUB, N_GRP).astype(jnp.int32)
    shifted = jnp.roll(ordering, -1, axis=0)
    corner_nodes = jnp.stack([ordering, shifted, jnp.roll(ordering, -1, axis=1), jnp.roll(shifted, -1, axis=1)], axis=-1)
    coarse_ids = corner_nodes[:, :, :, None] * DOF_NODE + jnp.arange(DOF_NODE, dtype=jnp.int32)[None, None, None, :]
    return coarse_ids.reshape(N_SUB, N_GRP, NCL).astype(jnp.int32)


def block_scale(own_key, extent, pieces, least, largest):
    level = 1.0
    for dim, blocks in pieces:
        steps = jax.random.uniform(jax.random.fold_in(jax.random.fold_in(own_key, 6), dim), (blocks,), jnp.float32, least / len(pieces), largest / len(pieces))
        level = level * jnp.repeat(jnp.exp(steps), extent[dim] // blocks).reshape((-1,) + (1,) * (len(extent) - 1 - dim))
    return level


def bell_draw(key, shape, width, most, cuts=(), kind=jnp.bfloat16):
    level = block_scale(key, shape, cuts, -0.22, 0.18) if cuts else 1.0
    drawn = jax.random.normal(key, shape, jnp.float32) * width * level
    return jnp.minimum(jnp.maximum(drawn, -most), most).astype(kind)


def setup_inputs(seed: int = 0) -> dict:
    key_of = jax.random.split(jax.random.key(seed), 8)
    applied_loads = draw_applied_loads(jax.random.fold_in(key_of[7], 71), 0)
    flex_matrix = draw_flex_matrix(jax.random.fold_in(key_of[7], 71), 0)
    schur_matrix = draw_schur_matrix(jax.random.fold_in(key_of[7], 71), 0)
    corner_coupling = bell_draw(key_of[3], (N_SUB, N_GRP, NCL, NI), (NI // 16) ** -0.5, 0.625, ((0, 16), (1, 16)), jnp.float32)
    coarse_inverse = draw_coarse_inverse(jax.random.fold_in(key_of[7], 71), 0)
    face_match = draw_face_match(jax.random.fold_in(key_of[7], 71), 0)
    corner_map = draw_corner_map(jax.random.fold_in(key_of[7], 71), 0)
    return dict(applied_loads=applied_loads, flex_matrix=flex_matrix, schur_matrix=schur_matrix, corner_coupling=corner_coupling, coarse_inverse=coarse_inverse, face_match=face_match, corner_map=corner_map)


def reorder(values, indices):
    return jnp.take_along_axis(values, jnp.broadcast_to(indices[:, :, None, :], values.shape), axis=3)


def neighbour_jump(displaced, matching):
    from_left_sub = reorder(jnp.roll(displaced[:, :, :, 1], 1, axis=0), matching[:, :, 0])
    from_right_sub = reorder(jnp.roll(displaced[:, :, :, 0], -1, axis=0), matching[:, :, 1])
    from_left_grp = reorder(jnp.roll(displaced[:, :, :, 3], 1, axis=1), matching[:, :, 2])
    from_right_grp = reorder(jnp.roll(displaced[:, :, :, 2], -1, axis=1), matching[:, :, 3])
    return jnp.stack([from_left_sub - displaced[:, :, :, 0], displaced[:, :, :, 1] - from_right_sub,
                      from_left_grp - displaced[:, :, :, 2], displaced[:, :, :, 3] - from_right_grp], axis=3)


def local_products(vectors, matrices):
    flat_vectors = vectors.reshape(N_SUB * N_GRP, LOADS, NI)
    flat_matrices = matrices.reshape(N_SUB * N_GRP, NI, NI)
    result = lax.map(lambda operands: jnp.dot(operands[0], operands[1], preferred_element_type=jnp.float32),
                     (flat_vectors, flat_matrices))
    return result.reshape(N_SUB, N_GRP, LOADS, NI)


def reference(applied_loads, flex_matrix, schur_matrix, corner_coupling, coarse_inverse, face_match, corner_map):
    highest = lax.Precision.HIGHEST
    layout = (N_SUB, N_GRP, LOADS, 4, FACE)
    face_signs = jnp.array([-1.0, 1.0, -1.0, 1.0], jnp.float32)[:, None]
    corner_flat = corner_map.reshape(-1)

    def apply_flex(direction):
        forces = (direction * face_signs).reshape(N_SUB, N_GRP, LOADS, NI)
        free = local_products(forces.astype(jnp.bfloat16), flex_matrix)
        corner = jnp.einsum('abkn,abjn->abkj', forces, corner_coupling, precision=highest)
        coarse_rhs = jnp.zeros((LOADS, NC), jnp.float32).at[:, corner_flat].add(
            jnp.transpose(corner, (2, 0, 1, 3)).reshape(LOADS, -1))
        lowered = jnp.dot(coarse_rhs, coarse_inverse.T, precision=highest)
        coarse_sol = jnp.dot(lowered, coarse_inverse, precision=highest)
        picked = jnp.transpose(coarse_sol[:, corner_flat].reshape(LOADS, N_SUB, N_GRP, NCL), (1, 2, 0, 3))
        displaced = free + jnp.einsum('abkj,abjn->abkn', picked, corner_coupling, precision=highest)
        curvature = jnp.sum(forces * displaced, axis=(0, 1, 3))
        return neighbour_jump(displaced.reshape(layout), face_match), curvature

    def apply_precond(current):
        weighted = (0.5 * current * face_signs).astype(jnp.bfloat16).reshape(N_SUB, N_GRP, LOADS, NI)
        response = local_products(weighted, schur_matrix)
        return 0.5 * neighbour_jump(response.reshape(layout), face_match)

    def inner(former, latter):
        return 0.5 * jnp.sum(former * latter, axis=(0, 1, 3, 4))

    right_side = neighbour_jump(applied_loads.reshape(layout), face_match)
    multipliers = jnp.zeros(layout, jnp.float32)
    residual = right_side
    precond = apply_precond(residual)
    precond_dot = inner(residual, precond)
    direction = precond
    for iteration in range(ITERS):
        image, curvature = apply_flex(direction)
        step_size = (precond_dot / curvature)[None, None, :, None, None]
        multipliers = multipliers + step_size * direction
        residual = residual - step_size * image
        if iteration + 1 < ITERS:
            precond = apply_precond(residual)
            next_dot = inner(residual, precond)
            direction = precond + (next_dot / precond_dot)[None, None, :, None, None] * direction
            precond_dot = next_dot
    return multipliers, residual
```

```python
import functools

import jax
import jax.numpy as jnp
from jax import lax
from jax.experimental import pallas as pl
from jax.experimental.pallas import tpu as pltpu
from jax.sharding import PartitionSpec as P

MESH = pl.DeviceIdType.MESH
F32 = jnp.float32
BF16 = jnp.bfloat16
OPPOSITE = (1, 0, 3, 2)
ANY = pl.BlockSpec(memory_space=pl.ANY)
VMEM = pl.BlockSpec(memory_space=pltpu.VMEM)
NT = (((1,), (1,)), ((), ()))


def dot(a, b):
    return jnp.dot(a, b, preferred_element_type=F32)


def dot_nt(a, b):
    return lax.dot_general(a, b, NT, preferred_element_type=F32)


def split(x):
    high = x.astype(BF16)
    return high, (x - high.astype(F32)).astype(BF16)


def stacked(x):
    return jnp.concatenate(split(x), axis=0)


def lane_chunks(x):
    total = x[:, 0:128]
    for c in range(1, x.shape[1] // 128):
        total = total + x[:, 128 * c : 128 * c + 128]
    return total


def kernel(
    n_sub, n_grp,
    loads_hbm, flex_hbm, schur_hbm, coupling_hbm, inverse_hbm, match_hbm, corner_hbm,
    mult_out, res_out,
    loads, flex, schur, coupling, inverse, match, corner, corner_pad,
    halo, near_coupling, near_corner,
    perm, wide_g, select, near_inverse, inv_hi, inv_lo,
    y_buf, free0, free1, res, z0, image0,
    dense, recv1, part, recv2, total, rhs,
    small, small_recv1, small2, small_recv2,
    local_sem, halo_send, halo_recv, near_send, near_recv,
    send1, rec1, send2, rec2, send3, rec3, ssend1, srec1, ssend2, srec2,
):
    s, g = lax.axis_index("sub"), lax.axis_index("grp")
    load_cases, interface = loads.shape
    face = interface // 4
    half = interface // 2
    size = inverse.shape[0]

    def sub_peer(d):
        return (lax.rem(s + d, n_sub), g)

    def grp_peer(d):
        return (s, lax.rem(g + d, n_grp))

    near = (sub_peer(n_sub - 1), sub_peer(1), grp_peer(n_grp - 1), grp_peer(1))

    def faces(f):
        return slice(face * f, face * f + face)

    def remote(src, dst, send, recv, to):
        copy = pltpu.make_async_remote_copy(
            src_ref=src, dst_ref=dst, send_sem=send, recv_sem=recv, device_id=to, device_id_type=MESH
        )
        copy.start()
        return copy

    barrier = pltpu.get_barrier_semaphore()
    for d in range(1, n_sub):
        pl.semaphore_signal(barrier, inc=1, device_id=sub_peer(d), device_id_type=MESH)
    for d in range(1, n_grp):
        pl.semaphore_signal(barrier, inc=1, device_id=grp_peer(d), device_id_type=MESH)

    sources = (
        (corner_hbm, corner), (loads_hbm.at[0, 0], loads), (match_hbm.at[0, 0], match),
        (coupling_hbm.at[0, 0], coupling), (schur_hbm.at[0, 0], schur), (inverse_hbm, inverse),
        (flex_hbm.at[0, 0], flex),
    )
    local = []
    for i, (src, dst) in enumerate(sources):
        copy = pltpu.make_async_copy(src, dst, local_sem.at[i])
        copy.start()
        local.append(copy)
    corner_copy, loads_copy, match_copy, coupling_copy, schur_copy, inverse_copy, flex_copy = local

    corner_copy.wait()
    corner_pad[...] = jnp.full(corner_pad.shape, -1, jnp.int32)
    corner_pad[0:1, 0 : corner.shape[2]] = corner[0]
    coupling_copy.wait()
    loads_copy.wait()
    pl.semaphore_wait(barrier, n_sub + n_grp - 2)

    pending = []

    def send_halo(step, f, src):
        copy = remote(
            src, halo.at[step, OPPOSITE[f]], halo_send.at[step, f], halo_recv.at[step, OPPOSITE[f]], near[f]
        )
        pending.append(copy)
        return copy

    arrivals = {}
    for f in range(4):
        arrivals[0, OPPOSITE[f]] = send_halo(0, f, loads.at[:, faces(f)])
    near_copies = []
    for f in range(4):
        o = OPPOSITE[f]
        near_copies.append(
            remote(coupling.at[:, faces(f)], near_coupling.at[o], near_send.at[0, f], near_recv.at[0, o], near[f])
        )
        near_copies.append(remote(corner_pad, near_corner.at[o], near_send.at[1, f], near_recv.at[1, o], near[f]))
    pending.extend(near_copies)

    match_copy.wait()
    row = lax.broadcasted_iota(jnp.int32, (face, face), 0)
    for f in range(4):
        perm[f] = (row == match[f : f + 1, :]).astype(BF16)

    def neighbour(step, f):
        arrivals[step, f].wait_recv()
        both = dot(stacked(halo[step, f]), perm[f])
        return both[:load_cases] + both[load_cases:]

    def send_out(step, f0, ref):
        for f in (f0, f0 + 1):
            arrivals[step, OPPOSITE[f]] = send_halo(step, f, ref.at[:, faces(f)])

    for f in range(4):
        res[:, faces(f)] = loads[:, faces(f)] - neighbour(0, f)

    def apply_schur(step):
        weighted = (0.5 * res[...]).astype(BF16)
        for h in range(2):
            cut = slice(half * h, half * h + half)
            y_buf[step // 2, :, cut] = dot(weighted, schur[:, cut])
            send_out(step, 2 * h, y_buf.at[step // 2])

    schur_copy.wait()
    apply_schur(1)

    for copy in near_copies:
        copy.wait_recv()
    wide_g[...] = jnp.zeros(wide_g.shape, BF16)
    own_hi, own_lo = split(coupling[...])
    corners = own_hi.shape[0]
    wide_g[0, 0:corners, :] = own_hi
    wide_g[1, 0:corners, :] = own_lo
    for f in range(4):
        hi, lo = split(near_coupling[f])
        wide_g[0, 16 * f + 16 : 16 * f + 16 + corners, faces(f)] = (-dot(hi, perm[f])).astype(BF16)
        wide_g[1, 16 * f + 16 : 16 * f + 16 + corners, faces(f)] = (-dot(lo, perm[f])).astype(BF16)
    lane = lax.broadcasted_iota(jnp.int32, (8, 128), 1)
    numbers = jnp.where(lane < corners, corner_pad[...], -1)
    for f in range(4):
        start = 16 * f + 16
        inside = jnp.logical_and(lane >= start, lane < start + corners)
        numbers = jnp.where(inside, pltpu.roll(near_corner[f], start, 1), numbers)
    column = jnp.broadcast_to(numbers.astype(F32)[0:1, :], (128, 128)).T
    unknown = lax.broadcasted_iota(jnp.int32, (128, size), 1).astype(F32)
    select[...] = (column[:, 0:1] == unknown).astype(BF16)

    def start_coarse(it, y):
        pair = dot_nt(stacked(0.5 * y), jnp.concatenate([wide_g[0], wide_g[1]], axis=0))
        mine = pair[:load_cases, :128] + pair[:load_cases, 128:] + pair[load_cases:, :128]
        spread = dot(stacked(mine), select[...])
        spread = spread[:load_cases] + spread[load_cases:]
        for t in range(n_sub):
            lg, h = t % 8, t // 8
            dense[it, t] = spread[8 * lg : 8 * lg + 8, size // 2 * h : size // 2 * h + size // 2]
        copies = []
        for d in range(1, n_sub):
            to = sub_peer(d)
            copies.append(
                remote(dense.at[it, to[0]], recv1.at[it, d], send1.at[it, d], rec1.at[it, d], to)
            )
        pending.extend(copies)
        return copies

    def middle_coarse(it, copies):
        acc = dense[it, s]
        for d in range(1, n_sub):
            copies[d - 1].wait_recv()
            acc = acc + recv1[it, d]
        part[it] = acc
        out = [
            remote(part.at[it], recv2.at[it, d], send2.at[it, d], rec2.at[it, d], grp_peer(d))
            for d in range(1, n_grp)
        ]
        pending.extend(out)
        return out

    def last_coarse(it, copies):
        acc = part[it]
        for d in range(1, n_grp):
            copies[d - 1].wait_recv()
            acc = acc + recv2[it, d]
        total[it] = acc
        rhs[it, s] = acc
        out = [
            remote(total.at[it], rhs.at[it, s], send3.at[it, d], rec3.at[it, d], sub_peer(d))
            for d in range(1, n_sub)
        ]
        pending.extend(out)
        return out

    def finish_coarse(it, copies):
        for copy in copies:
            copy.wait_recv()
        whole = jnp.concatenate(
            [
                jnp.concatenate([rhs[it, 8 * h + lg] for lg in range(8)], axis=0)
                for h in range(2)
            ],
            axis=1,
        )
        both = stacked(whole)
        pair = dot_nt(both, jnp.concatenate([near_inverse[0], near_inverse[1]], axis=0))
        picked = pair[:load_cases, :128] + pair[:load_cases, 128:] + pair[load_cases:, :128]
        low = dot_nt(both, inv_hi[...])
        low = low[:load_cases] + low[load_cases:] + dot_nt(both[:load_cases], inv_lo[...])
        return picked, low

    def spread_coarse(picked, f):
        both = stacked(picked)
        out = dot(both, wide_g[0, :, faces(f)])
        return out[:load_cases] + out[load_cases:] + dot(both[:load_cases], wide_g[1, :, faces(f)])

    def row_of(a, b):
        return jnp.sum(jnp.concatenate([a, b], axis=0).T, axis=0, keepdims=True)

    def start_small(it, rows):
        for i, r in enumerate(rows):
            small[it, i : i + 1, :] = r
        copies = [
            remote(small.at[it], small_recv1.at[it, d], ssend1.at[it, d], srec1.at[it, d], grp_peer(d))
            for d in range(1, n_grp)
        ]
        pending.extend(copies)
        return copies

    def middle_small(it, copies):
        acc = small[it]
        for d in range(1, n_grp):
            copies[d - 1].wait_recv()
            acc = acc + small_recv1[it, d]
        small2[it] = acc
        out = [
            remote(small2.at[it], small_recv2.at[it, d], ssend2.at[it, d], srec2.at[it, d], sub_peer(d))
            for d in range(1, n_sub)
        ]
        pending.extend(out)
        return out

    def finish_small(it, copies, count):
        acc = small2[it]
        for d in range(1, n_sub):
            copies[d - 1].wait_recv()
            acc = acc + small_recv2[it, d]
        out = []
        for i in range(count):
            turned = jnp.broadcast_to(acc[i : i + 1, :], (128, 128)).T
            out += [turned[:load_cases], turned[load_cases:]]
        return out

    def tile(a):
        return jnp.concatenate([a] * (face // 128), axis=1)

    small[...] = jnp.zeros(small.shape, F32)
    y0 = y_buf[0]
    coarse = start_coarse(0, y0)
    rz_lanes = lane_chunks(0.5 * res[...] * y0)

    for f in range(4):
        z0[:, faces(f)] = 0.5 * (y_buf[0, :, faces(f)] - neighbour(1, f))
    direction = z0[...].astype(BF16)
    flex_copy.wait()
    for h in range(2):
        cut = slice(half * h, half * h + half)
        free0[:, cut] = dot(direction, flex[:, cut])
        send_out(2, 2 * h, free0)
    little = start_small(0, [row_of(rz_lanes, lane_chunks(z0[...] * free0[...]))])
    coarse = middle_coarse(0, coarse)

    inverse_copy.wait()
    hi, lo = split(inverse[...])
    inv_hi[...] = hi
    inv_lo[...] = lo
    chosen_hi = dot_nt(select[...], inv_hi[...]).astype(BF16)
    chosen_lo = dot_nt(select[...], inv_lo[...]).astype(BF16)
    columns = (
        dot(chosen_hi, inv_hi[...]) + dot(chosen_lo, inv_hi[...]) + dot(chosen_hi, inv_lo[...])
    )
    hi, lo = split(columns)
    near_inverse[0] = hi
    near_inverse[1] = lo

    little = middle_small(0, little)
    for f in range(4):
        image0[:, faces(f)] = free0[:, faces(f)] - neighbour(2, f)
    coarse = last_coarse(0, coarse)
    rz0, free_curv = finish_small(0, little, 1)
    picked, low0 = finish_coarse(0, coarse)
    curv0 = free_curv + jnp.sum(low0 * low0, axis=1, keepdims=True)
    a0 = rz0 / curv0
    for f in range(4):
        image0[:, faces(f)] = image0[:, faces(f)] + spread_coarse(picked, f)
        res[:, faces(f)] = res[:, faces(f)] - tile(a0) * image0[:, faces(f)]

    apply_schur(3)
    y1 = y_buf[1]
    coarse = start_coarse(1, y1)
    rz_lanes = lane_chunks(0.5 * res[...] * y1)
    for f in range(4):
        mult_out[:, faces(f)] = 0.5 * (y_buf[1, :, faces(f)] - neighbour(3, f))
    direction = mult_out[...].astype(BF16)
    for h in range(2):
        cut = slice(half * h, half * h + half)
        free1[:, cut] = dot(direction, flex[:, cut])
        send_out(4, 2 * h, free1)
    z1 = mult_out[...]
    little = start_small(
        1,
        [
            row_of(rz_lanes, lane_chunks(z1 * free1[...])),
            row_of(lane_chunks(z1 * free0[...]), jnp.zeros((load_cases, 128), F32)),
        ],
    )
    coarse = middle_coarse(1, coarse)
    little = middle_small(1, little)
    for f in range(4):
        res_out[:, faces(f)] = free1[:, faces(f)] - neighbour(4, f)
    coarse = last_coarse(1, coarse)
    rz1, curv_11, curv_10, _ = finish_small(1, little, 2)
    picked, low1 = finish_coarse(1, coarse)
    beta = rz1 / rz0
    low = low1 + beta[:, 0:1] * low0
    curv1 = curv_11 + 2.0 * beta * curv_10 + beta * beta * free_curv + jnp.sum(low * low, axis=1, keepdims=True)
    a1 = rz1 / curv1
    for f in range(4):
        sign = 1.0 if f % 2 else -1.0
        image = res_out[:, faces(f)] + spread_coarse(picked, f) + tile(beta) * image0[:, faces(f)]
        res_out[:, faces(f)] = sign * (res[:, faces(f)] - tile(a1) * image)
        mult_out[:, faces(f)] = sign * (
            tile(a1) * mult_out[:, faces(f)] + tile(a0 + a1 * beta) * z0[:, faces(f)]
        )
    for copy in pending:
        copy.wait_send()


def solution(mesh):
    n_sub, n_grp = mesh.shape["sub"], mesh.shape["grp"]

    def shards(loads, flex, schur, coupling, inverse, match, corner):
        load_cases, interface = loads.shape[2:]
        face = interface // 4
        corners, size = coupling.shape[2], inverse.shape[0]
        vmem, dma = pltpu.VMEM, pltpu.SemaphoreType.DMA
        flat = (load_cases, interface)
        block = (8, size // 2)
        scratch = [
            vmem(flat, F32), vmem((interface, interface), BF16), vmem((interface, interface), BF16),
            vmem((corners, interface), F32), vmem((size, size), F32), vmem((4, face), jnp.int32),
            vmem(corner.shape, jnp.int32), vmem((8, 128), jnp.int32),
            vmem((5, 4, load_cases, face), F32), vmem((4, corners, face), F32), vmem((4, 8, 128), jnp.int32),
            vmem((4, face, face), BF16), vmem((2, 128, interface), BF16), vmem((128, size), BF16),
            vmem((2, 128, size), BF16), vmem((size, size), BF16), vmem((size, size), BF16),
            vmem((2,) + flat, F32), vmem(flat, F32), vmem(flat, F32), vmem(flat, F32), vmem(flat, F32),
            vmem(flat, F32),
            vmem((2, n_sub) + block, F32), vmem((2, n_sub) + block, F32), vmem((2,) + block, F32),
            vmem((2, n_grp) + block, F32), vmem((2,) + block, F32), vmem((2, n_sub) + block, F32),
            vmem((2, 8, 128), F32), vmem((2, n_grp, 8, 128), F32), vmem((2, 8, 128), F32),
            vmem((2, n_sub, 8, 128), F32),
            dma((7,)), dma((5, 4)), dma((5, 4)), dma((2, 4)), dma((2, 4)),
            dma((2, n_sub)), dma((2, n_sub)), dma((2, n_grp)), dma((2, n_grp)), dma((2, n_sub)), dma((2, n_sub)),
            dma((2, n_grp)), dma((2, n_grp)), dma((2, n_sub)), dma((2, n_sub)),
        ]
        out = pl.pallas_call(
            functools.partial(kernel, n_sub, n_grp),
            out_shape=(jax.ShapeDtypeStruct(flat, F32), jax.ShapeDtypeStruct(flat, F32)),
            in_specs=[ANY] * 7,
            out_specs=(VMEM, VMEM),
            scratch_shapes=scratch,
            compiler_params=pltpu.CompilerParams(
                collective_id=0, has_side_effects=True, vmem_limit_bytes=48 * 2**20
            ),
            name="cg",
        )(loads, flex, schur, coupling, inverse, match, corner)
        return tuple(x.reshape(1, 1, load_cases, 4, face) for x in out)

    split4 = P("sub", "grp", None, None)
    return jax.shard_map(
        shards,
        mesh=mesh,
        in_specs=(split4, split4, split4, split4, P(), split4, P("sub", "grp", None)),
        out_specs=(P("sub", "grp", None, None, None), P("sub", "grp", None, None, None)),
        check_vma=False,
    )
```

```python
import functools

import jax
import jax.numpy as jnp
from jax import lax
from jax.experimental import pallas as pl
from jax.experimental.pallas import tpu as pltpu
from jax.sharding import PartitionSpec as P

MESH = pl.DeviceIdType.MESH
F32 = jnp.float32
BF16 = jnp.bfloat16
OPPOSITE = (1, 0, 3, 2)
HBM = pl.BlockSpec(memory_space=pltpu.HBM)
VMEM = pl.BlockSpec(memory_space=pltpu.VMEM)
NT = (((1,), (1,)), ((), ()))
SIDE = 4
FAR_FIRST = sorted(range(1, 16), key=lambda k: -(2 - abs(2 - k // 4)) - (2 - abs(2 - k % 4)))
RING = (4, 3, 5, 2, 6, 1, 7)


def dot(a, b):
    return jnp.dot(a, b, preferred_element_type=F32)


def dot_nt(a, b):
    return lax.dot_general(a, b, NT, preferred_element_type=F32)


def split(x):
    high = x.astype(BF16)
    return high, (x - high.astype(F32)).astype(BF16)


def stacked(x):
    return jnp.concatenate(split(x), axis=0)


def lane_chunks(x):
    total = x[:, 0:128]
    for c in range(1, x.shape[1] // 128):
        total = total + x[:, 128 * c : 128 * c + 128]
    return total


def kernel(
    n_sub, n_grp,
    loads_hbm, flex_hbm, schur_hbm, coupling_hbm, inverse_hbm, match_hbm, corner_hbm,
    mult_out, res_out,
    loads, flex, schur, coupling, inverse, match, corner, corner_pad,
    halo, near_coupling, near_corner,
    perm, padded, wide_g, schur_g, select, near_inverse, inv_hi, inv_lo,
    res, y_buf, free, z_buf, image,
    dense, recv1, part, chip, pair, recv2, total, rhs,
    local_sem, halo_send, halo_recv, near_send, near_recv,
    send1, rec1, send2, rec2, send3, rec3,
):
    s, g = lax.axis_index("sub"), lax.axis_index("grp")
    load_cases, interface = loads.shape
    face = interface // 4
    half = interface // 2
    size = inverse.shape[0]
    width = size // 2
    plain, wide = slice(0, width), slice(0, width + 128)
    corners = coupling.shape[0]
    row, column = s // SIDE, lax.rem(s, SIDE)
    rows_on = [lax.rem(row + d, SIDE) * SIDE for d in range(SIDE)]
    columns_on = [lax.rem(column + d, SIDE) for d in range(SIDE)]

    def sub_peer(k):
        return (rows_on[k // SIDE] + columns_on[k % SIDE], g)

    def z_peer(d):
        return (s, lax.rem(g + 2 * d, n_grp))

    other = (s, g + 1 - 2 * lax.rem(g, 2))
    near = (
        (lax.rem(s + n_sub - 1, n_sub), g), (lax.rem(s + 1, n_sub), g),
        (s, lax.rem(g + n_grp - 1, n_grp)), (s, lax.rem(g + 1, n_grp)),
    )

    def faces(f):
        return slice(face * f, face * f + face)

    def remote(src, dst, send, recv, to):
        pltpu.make_async_remote_copy(
            src_ref=src, dst_ref=dst, send_sem=send, recv_sem=recv, device_id=to, device_id_type=MESH
        ).start()

    def drain(ref, sem):
        pltpu.make_async_copy(ref, ref, sem).wait()

    sent = []

    def flush():
        for ref, sem in sent:
            drain(ref, sem)
        sent.clear()

    barrier = pltpu.get_barrier_semaphore()
    for d in range(1, n_sub):
        to = (lax.rem(s + d, n_sub), g)
        pl.semaphore_signal(barrier, inc=1, device_id=to, device_id_type=MESH)
    for d in RING:
        pl.semaphore_signal(barrier, inc=1, device_id=z_peer(d), device_id_type=MESH)
    for d in (1, n_grp - 1):
        to = (s, lax.rem(g + d, n_grp))
        pl.semaphore_signal(barrier, inc=1, device_id=to, device_id_type=MESH)

    sources = (
        (corner_hbm, corner), (coupling_hbm.at[0], coupling), (loads_hbm.at[0, 0], loads),
        (match_hbm.at[0, 0], match), (schur_hbm.at[0, 0], schur), (flex_hbm.at[0, 0], flex), (inverse_hbm, inverse),
    )
    local = []
    for i, (src, dst) in enumerate(sources):
        copy = pltpu.make_async_copy(src, dst, local_sem.at[i])
        copy.start()
        local.append(copy)
    corner_copy, coupling_copy, loads_copy, match_copy, schur_copy, flex_copy, inverse_copy = local

    corner_copy.wait()
    corner_pad[...] = jnp.full(corner_pad.shape, -1, jnp.int32)
    corner_pad[0:1, 0:corners] = corner[0]
    coupling_copy.wait()
    loads_copy.wait()
    pl.semaphore_wait(barrier, n_sub - 1 + len(RING) + 2)

    for f in range(4):
        o = OPPOSITE[f]
        remote(coupling.at[:, :, faces(f)], near_coupling.at[o], near_send.at[0], near_recv.at[0], near[f])
    sent.append((near_coupling, near_send.at[0]))

    def send_out(step, f0, ref):
        for f in (f0, f0 + 1):
            o = OPPOSITE[f]
            remote(ref.at[:, faces(f)], halo.at[step, o], halo_send.at[step, f0 // 2], halo_recv.at[step, f0 // 2], near[f])
        sent.append((halo.at[step, f0 : f0 + 2], halo_send.at[step, f0 // 2]))

    send_out(0, 0, loads)
    send_out(0, 2, loads)
    for f in range(4):
        remote(corner_pad, near_corner.at[OPPOSITE[f]], near_send.at[1], near_recv.at[1], near[f])
    sent.append((near_corner, near_send.at[1]))

    match_copy.wait()
    index = lax.broadcasted_iota(jnp.int32, (face, face), 0)
    for f in range(4):
        perm[f] = (index == match[f : f + 1, :]).astype(BF16)

    def neighbour(step, f):
        if f % 2 == 0:
            drain(halo.at[step, f : f + 2], halo_recv.at[step, f // 2])
        both = dot(stacked(halo[step, f]), perm[f])
        return both[:load_cases] + both[load_cases:]

    wide_g[...] = jnp.zeros(wide_g.shape, BF16)
    padded[...] = jnp.zeros(padded.shape, F32)
    for k in range(corners):
        padded[k : k + 1, :] = coupling[k]
    hi, lo = split(padded[...])
    wide_g[0:16, :] = hi
    wide_g[128:144, :] = lo
    drain(near_coupling, near_recv.at[0])
    for f in range(4):
        for k in range(corners):
            padded[k : k + 1, faces(f)] = near_coupling[f, k]
        both = -dot(stacked(padded[:, faces(f)]), perm[f])
        start = 16 * f + 16
        wide_g[start : start + 16, faces(f)] = both[:16].astype(BF16)
        wide_g[start + 128 : start + 144, faces(f)] = both[16:].astype(BF16)
    schur_copy.wait()
    for f in range(4):
        both = dot_nt(schur[faces(f), :], wide_g[...])
        hi, lo = split(0.5 * (both[:, :128] + both[:, 128:]))
        schur_g[faces(f), 0:128] = hi
        schur_g[faces(f), 128:256] = lo

    drain(near_corner, near_recv.at[1])
    lane = lax.broadcasted_iota(jnp.int32, (8, 128), 1)
    numbers = jnp.where(lane < corners, corner_pad[...], -1)
    for f in range(4):
        start = 16 * f + 16
        inside = jnp.logical_and(lane >= start, lane < start + corners)
        numbers = jnp.where(inside, pltpu.roll(near_corner[f], start, 1), numbers)
    turned = jnp.broadcast_to(numbers.astype(F32)[0:1, :], (128, 128)).T
    unknown = lax.broadcasted_iota(jnp.int32, (128, size), 1).astype(F32)
    select[...] = (turned[:, 0:1] == unknown).astype(BF16)

    def start_coarse(it, both):
        spread = dot(stacked(both[:, :128] + both[:, 128:]), select[...])
        spread = spread[:load_cases] + spread[load_cases:]
        for t in range(n_sub):
            lg, h = t % 8, t // 8
            dense[it, t] = spread[8 * lg : 8 * lg + 8, width * h : width * h + width]
        for k in FAR_FIRST:
            to = sub_peer(k)
            remote(dense.at[it, to[0]], recv1.at[it, k - 1], send1.at[it], rec1.at[it], to)
        sent.append((recv1.at[it], send1.at[it]))

    def middle_coarse(it, cut):
        drain(recv1.at[it], rec1.at[it])
        acc = dense[it, s]
        for k in range(1, n_sub):
            acc = acc + recv1[it, k - 1]
        part[it, :, :width] = acc
        remote(part.at[it, :, cut], chip.at[it, :, cut], send2.at[it, 0], rec2.at[it, 0], other)
        sent.append((chip.at[it, :, cut], send2.at[it, 0]))

    def third_coarse(it, cut):
        drain(chip.at[it, :, cut], rec2.at[it, 0])
        pair[it, :, cut] = part[it, :, cut] + chip[it, :, cut]
        for d in RING:
            remote(pair.at[it, :, cut], recv2.at[it, d - 1, :, cut], send2.at[it, 1], rec2.at[it, 1], z_peer(d))
        sent.append((recv2.at[it, :, :, cut], send2.at[it, 1]))

    def last_coarse(it, cut):
        drain(recv2.at[it, :, :, cut], rec2.at[it, 1])
        acc = pair[it, :, cut]
        for d in RING:
            acc = acc + recv2[it, d - 1, :, cut]
        total[it, :, cut] = acc
        rhs[it, s, :, cut] = acc
        for k in FAR_FIRST:
            remote(total.at[it, :, cut], rhs.at[it, s, :, cut], send3.at[it], rec3.at[it], sub_peer(k))
        sent.append((rhs.at[it, 0 : n_sub - 1, :, cut], send3.at[it]))

    def whole_coarse(it, cut):
        drain(rhs.at[it, 0 : n_sub - 1, :, cut], rec3.at[it])
        return stacked(
            jnp.concatenate(
                [
                    jnp.concatenate([rhs[it, 8 * h + lg, :, :width] for lg in range(8)], axis=0)
                    for h in range(2)
                ],
                axis=1,
            )
        )

    def pick(both):
        out = dot_nt(both, near_inverse[...])
        return out[:load_cases, :128] + out[:load_cases, 128:] + out[load_cases:, :128]

    def lowered(both):
        low = dot_nt(both, inv_hi[...])
        return low[:load_cases] + low[load_cases:] + dot_nt(both[:load_cases], inv_lo[...])

    def spread_coarse(both, f):
        out = dot(both, wide_g[0:128, faces(f)])
        return out[:load_cases] + out[load_cases:] + dot(both[:load_cases], wide_g[128:256, faces(f)])

    def row_of(a, b):
        return jnp.sum(jnp.concatenate([a, b], axis=0).T, axis=0, keepdims=True)

    def tile(a):
        return jnp.concatenate([a] * (face // 128), axis=1)

    def apply_schur(it, weighted):
        for h in range(2):
            cut = slice(half * h, half * h + half)
            y_buf[it, :, cut] = dot(weighted, schur[:, cut])
            send_out(2 * it + 1, 2 * h, y_buf.at[it])

    def start_flex(it):
        for f in (2, 3):
            z_buf[it, :, faces(f)] = 0.5 * (y_buf[it, :, faces(f)] - neighbour(2 * it + 1, f))
        free[it] = dot(z_buf[it, :, half:].astype(BF16), flex[half:, :])

    def finish_flex(it):
        for f in (0, 1):
            z_buf[it, :, faces(f)] = 0.5 * (y_buf[it, :, faces(f)] - neighbour(2 * it + 1, f))
        direction = z_buf[it, :, :half].astype(BF16)
        for h in range(2):
            cut = slice(half * h, half * h + half)
            free[it, :, cut] = free[it, :, cut] + dot(direction, flex[:half, cut])
            send_out(2 * it + 2, 2 * h, free.at[it])

    for f in (2, 3):
        res[:, faces(f)] = loads[:, faces(f)] - neighbour(0, f)
    both = dot((0.5 * res[:, half:]).astype(BF16), schur_g[half:, :])
    for f in (0, 1):
        res[:, faces(f)] = loads[:, faces(f)] - neighbour(0, f)
    weighted = (0.5 * res[...]).astype(BF16)
    start_coarse(0, both + dot(weighted[:, :half], schur_g[:half, :]))
    apply_schur(0, weighted)

    inverse_copy.wait()
    hi, lo = split(inverse[...])
    inv_hi[...] = hi
    inv_lo[...] = lo
    chosen_hi = dot_nt(select[...], inv_hi[...]).astype(BF16)
    chosen_lo = dot_nt(select[...], inv_lo[...]).astype(BF16)
    hi, lo = split(dot(chosen_hi, inv_hi[...]) + dot(chosen_lo, inv_hi[...]) + dot(chosen_hi, inv_lo[...]))
    near_inverse[0:128, :] = hi
    near_inverse[128:256, :] = lo
    flex_copy.wait()

    middle_coarse(0, plain)
    start_flex(0)
    third_coarse(0, plain)
    finish_flex(0)
    rows = [row_of(lane_chunks(0.5 * res[...] * y_buf[0]), lane_chunks(z_buf[0] * free[0]))]
    flush()
    last_coarse(0, plain)
    for f in range(4):
        image[0, :, faces(f)] = free[0, :, faces(f)] - neighbour(2, f)
    both_rhs = whole_coarse(0, plain)
    both = stacked(pick(both_rhs))
    for f in range(4):
        image[0, :, faces(f)] = image[0, :, faces(f)] + spread_coarse(both, f)

    weighted = (0.5 * image[0]).astype(BF16)
    apply_schur(1, weighted)
    start_coarse(1, dot(weighted, schur_g[...]))
    low0 = lowered(both_rhs)
    rows.append(
        row_of(
            lane_chunks(0.5 * (image[0] * y_buf[0] + res[...] * y_buf[1])),
            lane_chunks(0.5 * image[0] * y_buf[1]),
        )
    )
    part[1, :, width:] = jnp.zeros((8, 128), F32)
    flush()
    start_flex(1)
    finish_flex(1)
    rows.append(
        row_of(
            lane_chunks(z_buf[1] * free[0] + z_buf[0] * free[1]),
            lane_chunks(z_buf[1] * free[1]),
        )
    )
    for i, r in enumerate(rows):
        part[1, i : i + 1, width:] = r
    middle_coarse(1, wide)
    third_coarse(1, wide)
    for f in range(4):
        image[1, :, faces(f)] = free[1, :, faces(f)] - neighbour(4, f)
    flush()
    last_coarse(1, wide)
    flush()
    both_rhs = whole_coarse(1, wide)
    both = stacked(pick(both_rhs))
    low1 = lowered(both_rhs)

    acc = rhs[1, 0, :, width:]
    for k in range(1, n_sub):
        acc = acc + rhs[1, k, :, width:]
    sums = []
    for i in range(len(rows)):
        turned = jnp.broadcast_to(acc[i : i + 1, :], (128, 128)).T
        sums += [turned[:load_cases], turned[load_cases:]]
    rz0, free_00, res_01, res_11, free_01, free_11 = sums
    a0 = rz0 / (free_00 + jnp.sum(low0 * low0, axis=1, keepdims=True))
    rz1 = rz0 - a0 * res_01 + a0 * a0 * res_11
    more = 1.0 + rz1 / rz0
    low = more[:, 0:1] * low0 - a0[:, 0:1] * low1
    curvature = (
        more * more * free_00 - more * a0 * free_01 + a0 * a0 * free_11 + jnp.sum(low * low, axis=1, keepdims=True)
    )
    a1 = rz1 / curvature
    first, second = a0 + a1 * more, a0 * a1
    for f in range(4):
        sign = 1.0 if f % 2 else -1.0
        one, two = tile(sign * first), tile(sign * second)
        mult_out[:, faces(f)] = one * z_buf[0, :, faces(f)] - two * z_buf[1, :, faces(f)]
        res_out[:, faces(f)] = (
            sign * res[:, faces(f)]
            - one * image[0, :, faces(f)]
            + two * (image[1, :, faces(f)] + spread_coarse(both, f))
        )


def solution(mesh):
    n_sub, n_grp = mesh.shape["sub"], mesh.shape["grp"]

    def shards(loads, flex, schur, coupling, inverse, match, corner):
        load_cases, interface = loads.shape[2:]
        face = interface // 4
        corners, size = coupling.shape[2], inverse.shape[0]
        vmem, dma = pltpu.VMEM, pltpu.SemaphoreType.DMA
        flat = (load_cases, interface)
        block, wide = (8, size // 2), (8, size // 2 + 128)
        scratch = [
            vmem(flat, F32), vmem((interface, interface), BF16), vmem((interface, interface), BF16),
            vmem((corners, 1, interface), F32), vmem((size, size), F32), vmem((4, face), jnp.int32),
            vmem(corner.shape, jnp.int32), vmem((8, 128), jnp.int32),
            vmem((5, 4, load_cases, face), F32), vmem((4, corners, 1, face), F32), vmem((4, 8, 128), jnp.int32),
            vmem((4, face, face), BF16), vmem((16, interface), F32), vmem((256, interface), BF16),
            vmem((interface, 256), BF16), vmem((128, size), BF16),
            vmem((256, size), BF16), vmem((size, size), BF16), vmem((size, size), BF16),
            vmem(flat, F32), vmem((2,) + flat, F32), vmem((2,) + flat, F32), vmem((2,) + flat, F32),
            vmem((2,) + flat, F32),
            vmem((2, n_sub) + block, F32), vmem((2, n_sub - 1) + block, F32), vmem((2,) + wide, F32),
            vmem((2,) + wide, F32), vmem((2,) + wide, F32), vmem((2, len(RING)) + wide, F32), vmem((2,) + wide, F32),
            vmem((2, n_sub) + wide, F32),
            dma((7,)), dma((5, 2)), dma((5, 2)), dma((2,)), dma((2,)),
            dma((2,)), dma((2,)), dma((2, 2)), dma((2, 2)), dma((2,)), dma((2,)),
        ]
        out = pl.pallas_call(
            functools.partial(kernel, n_sub, n_grp),
            out_shape=(jax.ShapeDtypeStruct(flat, F32), jax.ShapeDtypeStruct(flat, F32)),
            in_specs=[HBM] * 7,
            out_specs=(VMEM, VMEM),
            scratch_shapes=scratch,
            compiler_params=pltpu.CompilerParams(
                collective_id=0, has_side_effects=True, vmem_limit_bytes=48 * 2**20
            ),
            name="cg",
        )(
            *(
                pltpu.with_memory_space_constraint(x, pltpu.HBM)
                for x in (loads, flex, schur, coupling.transpose(0, 2, 1, 3), inverse, match, corner)
            )
        )
        return tuple(x.reshape(1, 1, load_cases, 4, face) for x in out)

    split4 = P("sub", "grp", None, None)
    return jax.shard_map(
        shards,
        mesh=mesh,
        in_specs=(split4, split4, split4, split4, P(), split4, P("sub", "grp", None)),
        out_specs=(P("sub", "grp", None, None, None), P("sub", "grp", None, None, None)),
        check_vma=False,
    )
```

```python
import functools

import jax
import jax.numpy as jnp
from jax import lax
from jax.experimental import pallas as pl
from jax.experimental.pallas import tpu as pltpu
from jax.sharding import PartitionSpec as P

MESH = pl.DeviceIdType.MESH
F32 = jnp.float32
BF16 = jnp.bfloat16
OPPOSITE = (1, 0, 3, 2)
HBM = pl.BlockSpec(memory_space=pltpu.HBM)
VMEM = pl.BlockSpec(memory_space=pltpu.VMEM)
NT = (((1,), (1,)), ((), ()))
SIDE = 4
FAR_FIRST = sorted(range(1, 16), key=lambda k: -(2 - abs(2 - k // 4)) - (2 - abs(2 - k % 4)))
RING = (4, 3, 5, 2, 6, 1, 7)


def dot(a, b):
    return jnp.dot(a, b, preferred_element_type=F32)


def dot_nt(a, b):
    return lax.dot_general(a, b, NT, preferred_element_type=F32)


def split(x):
    high = x.astype(BF16)
    return high, (x - high.astype(F32)).astype(BF16)


def stacked(x):
    return jnp.concatenate(split(x), axis=0)


def lane_chunks(x):
    total = x[:, 0:128]
    for c in range(1, x.shape[1] // 128):
        total = total + x[:, 128 * c : 128 * c + 128]
    return total


def kernel(
    n_sub, n_grp,
    loads_hbm, flex_hbm, schur_hbm, coupling_hbm, inverse_hbm, match_hbm, corner_hbm,
    out,
    loads, flex, schur, coupling, inverse, match, corner, corner_pad,
    halo, near_coupling, near_corner,
    perm, padded, wide_g, schur_g, g_schur, g_schur_g, select, near_inverse, inv_hi, inv_lo,
    res, y_buf, free, z_buf, image,
    dense, recv1, part, chip, pair, recv2, total, rhs,
    local_sem, halo_send, halo_recv, near_send, near_recv,
    send1, rec1, send2, rec2, send3, rec3,
):
    s, g = lax.axis_index("sub"), lax.axis_index("grp")
    load_cases, interface = loads.shape
    face = interface // 4
    half = interface // 2
    size = inverse.shape[0]
    width = size // 2
    plain, wide = slice(0, width), slice(0, width + 128)
    corners = coupling.shape[0]
    row, column = s // SIDE, lax.rem(s, SIDE)
    rows_on = [lax.rem(row + d, SIDE) * SIDE for d in range(SIDE)]
    columns_on = [lax.rem(column + d, SIDE) for d in range(SIDE)]

    def sub_peer(k):
        return (rows_on[k // SIDE] + columns_on[k % SIDE], g)

    def z_peer(d):
        return (s, lax.rem(g + 2 * d, n_grp))

    other = (s, g + 1 - 2 * lax.rem(g, 2))
    near = (
        (lax.rem(s + n_sub - 1, n_sub), g), (lax.rem(s + 1, n_sub), g),
        (s, lax.rem(g + n_grp - 1, n_grp)), (s, lax.rem(g + 1, n_grp)),
    )

    def faces(f):
        return slice(face * f, face * f + face)

    def remote(src, dst, send, recv, to):
        pltpu.make_async_remote_copy(
            src_ref=src, dst_ref=dst, send_sem=send, recv_sem=recv, device_id=to, device_id_type=MESH
        ).start()

    def drain(ref, sem):
        pltpu.make_async_copy(ref, ref, sem).wait()

    sent = []

    def flush():
        for ref, sem in sent:
            drain(ref, sem)
        sent.clear()

    barrier = pltpu.get_barrier_semaphore()
    for d in range(1, n_sub):
        to = (lax.rem(s + d, n_sub), g)
        pl.semaphore_signal(barrier, inc=1, device_id=to, device_id_type=MESH)
    for d in RING:
        pl.semaphore_signal(barrier, inc=1, device_id=z_peer(d), device_id_type=MESH)
    for d in (1, n_grp - 1):
        to = (s, lax.rem(g + d, n_grp))
        pl.semaphore_signal(barrier, inc=1, device_id=to, device_id_type=MESH)

    sources = (
        (corner_hbm, corner), (coupling_hbm.at[0], coupling), (loads_hbm.at[0, 0], loads),
        (match_hbm.at[0, 0], match), (schur_hbm.at[0, 0], schur), (flex_hbm.at[0, 0], flex), (inverse_hbm, inverse),
    )
    local = []
    for i, (src, dst) in enumerate(sources):
        copy = pltpu.make_async_copy(src, dst, local_sem.at[i])
        copy.start()
        local.append(copy)
    corner_copy, coupling_copy, loads_copy, match_copy, schur_copy, flex_copy, inverse_copy = local

    corner_copy.wait()
    corner_pad[...] = jnp.full(corner_pad.shape, -1, jnp.int32)
    corner_pad[0:1, 0:corners] = corner[0]
    coupling_copy.wait()
    loads_copy.wait()
    pl.semaphore_wait(barrier, n_sub - 1 + len(RING) + 2)

    for f in range(4):
        o = OPPOSITE[f]
        remote(coupling.at[:, :, faces(f)], near_coupling.at[o], near_send.at[0], near_recv.at[0], near[f])
    for f in range(4):
        remote(corner_pad, near_corner.at[OPPOSITE[f]], near_send.at[1], near_recv.at[1], near[f])
    sent.append((near_coupling, near_send.at[0]))
    sent.append((near_corner, near_send.at[1]))

    def send_out(step, f0, ref):
        for f in (f0, f0 + 1):
            o = OPPOSITE[f]
            remote(ref.at[:, faces(f)], halo.at[step, o], halo_send.at[step, f0 // 2], halo_recv.at[step, f0 // 2], near[f])
        sent.append((halo.at[step, f0 : f0 + 2], halo_send.at[step, f0 // 2]))

    send_out(0, 0, loads)
    send_out(0, 2, loads)
    match_copy.wait()
    index = lax.broadcasted_iota(jnp.int32, (face, face), 0)
    for f in range(4):
        perm[f] = (index == match[f : f + 1, :]).astype(BF16)

    def neighbour(step, f):
        if f % 2 == 0:
            drain(halo.at[step, f : f + 2], halo_recv.at[step, f // 2])
        both = dot(stacked(halo[step, f]), perm[f])
        return both[:load_cases] + both[load_cases:]

    wide_g[...] = jnp.zeros(wide_g.shape, BF16)
    padded[...] = jnp.zeros(padded.shape, F32)
    for k in range(corners):
        padded[k : k + 1, :] = coupling[k]
    hi, lo = split(padded[...])
    wide_g[0:16, :] = hi
    wide_g[128:144, :] = lo
    drain(near_coupling, near_recv.at[0])
    for f in range(4):
        for k in range(corners):
            padded[k : k + 1, faces(f)] = near_coupling[f, k]
        both = -dot(stacked(padded[:, faces(f)]), perm[f])
        start = 16 * f + 16
        wide_g[start : start + 16, faces(f)] = both[:16].astype(BF16)
        wide_g[start + 128 : start + 144, faces(f)] = both[16:].astype(BF16)
    drain(near_corner, near_recv.at[1])
    lane = lax.broadcasted_iota(jnp.int32, (8, 128), 1)
    numbers = jnp.where(lane < corners, corner_pad[...], -1)
    for f in range(4):
        start = 16 * f + 16
        inside = jnp.logical_and(lane >= start, lane < start + corners)
        numbers = jnp.where(inside, pltpu.roll(near_corner[f], start, 1), numbers)
    turned = jnp.broadcast_to(numbers.astype(F32)[0:1, :], (128, 128)).T
    unknown = lax.broadcasted_iota(jnp.int32, (128, size), 1).astype(F32)
    select[...] = (turned[:, 0:1] == unknown).astype(BF16)
    schur_copy.wait()
    for f in range(4):
        both = dot_nt(schur[faces(f), :], wide_g[...])
        hi, lo = split(0.5 * (both[:, :128] + both[:, 128:]))
        schur_g[faces(f), 0:128] = hi
        schur_g[faces(f), 128:256] = lo

    def start_coarse(it, mine):
        spread = dot(stacked(mine), select[...])
        spread = spread[:load_cases] + spread[load_cases:]
        for t in range(n_sub):
            lg, h = t % 8, t // 8
            dense[it, t] = spread[8 * lg : 8 * lg + 8, width * h : width * h + width]
        for k in FAR_FIRST:
            to = sub_peer(k)
            remote(dense.at[it, to[0]], recv1.at[it, k - 1], send1.at[it], rec1.at[it], to)
        sent.append((recv1.at[it], send1.at[it]))

    def middle_coarse(it, cut):
        drain(recv1.at[it], rec1.at[it])
        acc = dense[it, s]
        for k in range(1, n_sub):
            acc = acc + recv1[it, k - 1]
        part[it, :, :width] = acc
        remote(part.at[it, :, cut], chip.at[it, :, cut], send2.at[it, 0], rec2.at[it, 0], other)
        sent.append((chip.at[it, :, cut], send2.at[it, 0]))

    def third_coarse(it, cut):
        drain(chip.at[it, :, cut], rec2.at[it, 0])
        pair[it, :, cut] = part[it, :, cut] + chip[it, :, cut]
        for d in RING:
            remote(pair.at[it, :, cut], recv2.at[it, d - 1, :, cut], send2.at[it, 1], rec2.at[it, 1], z_peer(d))
        sent.append((recv2.at[it, :, :, cut], send2.at[it, 1]))

    def last_coarse(it, cut):
        drain(recv2.at[it, :, :, cut], rec2.at[it, 1])
        acc = pair[it, :, cut]
        for d in RING:
            acc = acc + recv2[it, d - 1, :, cut]
        total[it, :, cut] = acc
        rhs[it, s, :, cut] = acc
        for k in FAR_FIRST:
            remote(total.at[it, :, cut], rhs.at[it, s, :, cut], send3.at[it], rec3.at[it], sub_peer(k))
        sent.append((rhs.at[it, 0 : n_sub - 1, :, cut], send3.at[it]))

    def whole_coarse(it, cut):
        drain(rhs.at[it, 0 : n_sub - 1, :, cut], rec3.at[it])
        return stacked(
            jnp.concatenate(
                [
                    jnp.concatenate([rhs[it, 8 * h + lg, :, :width] for lg in range(8)], axis=0)
                    for h in range(2)
                ],
                axis=1,
            )
        )

    def pick(both):
        out = dot(both, near_inverse[...])
        return out[:load_cases, :128] + out[:load_cases, 128:] + out[load_cases:, :128]

    def lowered(both):
        low = dot(both, inv_hi[...])
        return low[:load_cases] + low[load_cases:] + dot(both[:load_cases], inv_lo[...])

    def twice(both, matrix, cut):
        out = dot(both, matrix[0:128, cut])
        return out[:load_cases] + out[load_cases:] + dot(both[:load_cases], matrix[128:256, cut])

    def row_of(a, b):
        return jnp.sum(jnp.concatenate([a, b], axis=0).T, axis=0, keepdims=True)

    def tile(a):
        return jnp.concatenate([a] * (face // 128), axis=1)

    def start_flex(it):
        for f in (2, 3):
            z_buf[it, :, faces(f)] = 0.5 * (y_buf[it, :, faces(f)] - neighbour(2 * it + 1, f))
        free[it] = dot(z_buf[it, :, half:].astype(BF16), flex[half:, :])

    def finish_flex(it):
        for f in (0, 1):
            z_buf[it, :, faces(f)] = 0.5 * (y_buf[it, :, faces(f)] - neighbour(2 * it + 1, f))
        direction = z_buf[it, :, :half].astype(BF16)
        for h in range(2):
            cut = slice(half * h, half * h + half)
            free[it, :, cut] = free[it, :, cut] + dot(direction, flex[:half, cut])
            send_out(2 * it + 2, 2 * h, free.at[it])

    for f in (2, 3):
        res[:, faces(f)] = loads[:, faces(f)] - neighbour(0, f)
    both = dot((0.5 * res[:, half:]).astype(BF16), schur_g[half:, :])
    for f in (0, 1):
        res[:, faces(f)] = loads[:, faces(f)] - neighbour(0, f)
    weighted = (0.5 * res[...]).astype(BF16)
    both = both + dot(weighted[:, :half], schur_g[:half, :])
    start_coarse(0, both[:, :128] + both[:, 128:])
    for h in range(2):
        cut = slice(half * h, half * h + half)
        y_buf[0, :, cut] = dot(weighted, schur[:, cut])
        send_out(1, 2 * h, y_buf.at[0])

    inverse_copy.wait()
    hi, lo = split(inverse[...].T)
    inv_hi[...] = hi
    inv_lo[...] = lo
    flex_copy.wait()

    middle_coarse(0, plain)
    start_flex(0)
    third_coarse(0, plain)
    finish_flex(0)
    rows = [row_of(lane_chunks(0.5 * res[...] * y_buf[0]), lane_chunks(z_buf[0] * free[0]))]

    for f in range(4):
        both = dot(wide_g[...], schur[:, faces(f)])
        hi, lo = split(0.5 * (both[:128] + both[128:]))
        g_schur[0:128, faces(f)] = hi
        g_schur[128:256, faces(f)] = lo
    both = dot(wide_g[...], schur_g[...])
    hi, lo = split(0.5 * (both[:128, :128] + both[:128, 128:] + both[128:, :128]))
    g_schur_g[0:128, :] = hi
    g_schur_g[128:256, :] = lo
    flush()
    last_coarse(0, plain)
    for f in range(4):
        image[0, :, faces(f)] = free[0, :, faces(f)] - neighbour(2, f)
    weighted = (0.5 * image[0]).astype(BF16)
    y_buf[1] = dot(weighted, schur[...])
    both = dot(weighted, schur_g[...])
    mine = both[:, :128] + both[:, 128:]
    chosen_hi = dot(select[...], inv_hi[...]).astype(BF16)
    chosen_lo = dot(select[...], inv_lo[...]).astype(BF16)
    both = dot_nt(inv_hi[...], jnp.concatenate([chosen_hi, chosen_lo], axis=0))
    hi, lo = split(both[:, :128] + both[:, 128:] + dot_nt(inv_lo[...], chosen_hi))
    near_inverse[:, 0:128] = hi
    near_inverse[:, 128:256] = lo
    both_rhs = whole_coarse(0, plain)
    both = stacked(pick(both_rhs))

    for h in range(2):
        cut = slice(half * h, half * h + half)
        y_buf[1, :, cut] = y_buf[1, :, cut] + twice(both, g_schur, cut)
        send_out(3, 2 * h, y_buf.at[1])
    start_coarse(1, mine + twice(both, g_schur_g, slice(0, 128)))
    for f in range(4):
        image[0, :, faces(f)] = image[0, :, faces(f)] + twice(both, wide_g, faces(f))
    low0 = lowered(both_rhs)
    rows.append(
        row_of(
            lane_chunks(0.5 * (image[0] * y_buf[0] + res[...] * y_buf[1])),
            lane_chunks(0.5 * image[0] * y_buf[1]),
        )
    )
    part[1, :, width:] = jnp.zeros((8, 128), F32)
    flush()
    start_flex(1)
    finish_flex(1)
    rows.append(row_of(lane_chunks(2.0 * z_buf[1] * free[0]), lane_chunks(z_buf[1] * free[1])))
    for i, r in enumerate(rows):
        part[1, i : i + 1, width:] = r
    middle_coarse(1, wide)
    third_coarse(1, wide)
    for f in range(4):
        image[1, :, faces(f)] = free[1, :, faces(f)] - neighbour(4, f)
    flush()
    last_coarse(1, wide)
    flush()
    both_rhs = whole_coarse(1, wide)
    both = stacked(pick(both_rhs))
    low1 = lowered(both_rhs)

    acc = rhs[1, 0, :, width:]
    for k in range(1, n_sub):
        acc = acc + rhs[1, k, :, width:]
    sums = []
    for i in range(len(rows)):
        turned = jnp.broadcast_to(acc[i : i + 1, :], (128, 128)).T
        sums += [turned[:load_cases], turned[load_cases:]]
    rz0, free_00, res_01, res_11, free_01, free_11 = sums
    a0 = rz0 / (free_00 + jnp.sum(low0 * low0, axis=1, keepdims=True))
    rz1 = rz0 - a0 * res_01 + a0 * a0 * res_11
    more = 1.0 + rz1 / rz0
    low = more[:, 0:1] * low0 - a0[:, 0:1] * low1
    curvature = (
        more * more * free_00 - more * a0 * free_01 + a0 * a0 * free_11 + jnp.sum(low * low, axis=1, keepdims=True)
    )
    a1 = rz1 / curvature
    first, second = a0 + a1 * more, a0 * a1
    for f in range(4):
        sign = 1.0 if f % 2 else -1.0
        one, two = tile(sign * first), tile(sign * second)
        out[:, f, :] = one * z_buf[0, :, faces(f)] - two * z_buf[1, :, faces(f)]
        out[:, f + 4, :] = (
            sign * res[:, faces(f)]
            - one * image[0, :, faces(f)]
            + two * (image[1, :, faces(f)] + twice(both, wide_g, faces(f)))
        )


def solution(mesh):
    n_sub, n_grp = mesh.shape["sub"], mesh.shape["grp"]

    def shards(loads, flex, schur, coupling, inverse, match, corner):
        load_cases, interface = loads.shape[2:]
        face = interface // 4
        corners, size = coupling.shape[2], inverse.shape[0]
        vmem, dma = pltpu.VMEM, pltpu.SemaphoreType.DMA
        flat = (load_cases, interface)
        block, wide = (8, size // 2), (8, size // 2 + 128)
        scratch = [
            vmem(flat, F32), vmem((interface, interface), BF16), vmem((interface, interface), BF16),
            vmem((corners, 1, interface), F32), vmem((size, size), F32), vmem((4, face), jnp.int32),
            vmem(corner.shape, jnp.int32), vmem((8, 128), jnp.int32),
            vmem((5, 4, load_cases, face), F32), vmem((4, corners, 1, face), F32), vmem((4, 8, 128), jnp.int32),
            vmem((4, face, face), BF16), vmem((16, interface), F32), vmem((256, interface), BF16),
            vmem((interface, 256), BF16), vmem((256, interface), BF16), vmem((256, 128), BF16), vmem((128, size), BF16),
            vmem((size, 256), BF16), vmem((size, size), BF16), vmem((size, size), BF16),
            vmem(flat, F32), vmem((2,) + flat, F32), vmem((2,) + flat, F32), vmem((2,) + flat, F32),
            vmem((2,) + flat, F32),
            vmem((2, n_sub) + block, F32), vmem((2, n_sub - 1) + block, F32), vmem((2,) + wide, F32),
            vmem((2,) + wide, F32), vmem((2,) + wide, F32), vmem((2, len(RING)) + wide, F32), vmem((2,) + wide, F32),
            vmem((2, n_sub) + wide, F32),
            dma((7,)), dma((5, 2)), dma((5, 2)), dma((2,)), dma((2,)),
            dma((2,)), dma((2,)), dma((2, 2)), dma((2, 2)), dma((2,)), dma((2,)),
        ]
        out = pl.pallas_call(
            functools.partial(kernel, n_sub, n_grp),
            out_shape=jax.ShapeDtypeStruct((load_cases, 8, face), F32),
            in_specs=[HBM] * 7,
            out_specs=VMEM,
            scratch_shapes=scratch,
            compiler_params=pltpu.CompilerParams(
                collective_id=0, has_side_effects=True, vmem_limit_bytes=48 * 2**20
            ),
            name="cg",
        )(
            *(
                pltpu.with_memory_space_constraint(x, pltpu.HBM)
                for x in (loads, flex, schur, coupling.transpose(0, 2, 1, 3), inverse, match, corner)
            )
        )
        out = out[None, None]
        return out[:, :, :, :4], out[:, :, :, 4:]

    split4 = P("sub", "grp", None, None)
    return jax.shard_map(
        shards,
        mesh=mesh,
        in_specs=(split4, split4, split4, split4, P(), split4, P("sub", "grp", None)),
        out_specs=(P("sub", "grp", None, None, None), P("sub", "grp", None, None, None)),
        check_vma=False,
    )
```

```python
import functools

import jax
import jax.numpy as jnp
from jax import lax
from jax.experimental import pallas as pl
from jax.experimental.pallas import tpu as pltpu
from jax.sharding import PartitionSpec as P

MESH = pl.DeviceIdType.MESH
F32 = jnp.float32
BF16 = jnp.bfloat16
OPPOSITE = (1, 0, 3, 2)
HBM = pl.BlockSpec(memory_space=pltpu.HBM)
VMEM = pl.BlockSpec(memory_space=pltpu.VMEM)
NT = (((1,), (1,)), ((), ()))
SIDE = 4
FAR_FIRST = sorted(range(1, 16), key=lambda k: -(2 - abs(2 - k // 4)) - (2 - abs(2 - k % 4)))
RING = (4, 3, 5, 2, 6, 1, 7)


def dot(a, b):
    return jnp.dot(a, b, preferred_element_type=F32)


def dot_nt(a, b):
    return lax.dot_general(a, b, NT, preferred_element_type=F32)


def split(x):
    high = x.astype(BF16)
    return high, (x - high.astype(F32)).astype(BF16)


def stacked(x):
    return jnp.concatenate(split(x), axis=0)


def lane_chunks(x):
    total = x[:, 0:128]
    for c in range(1, x.shape[1] // 128):
        total = total + x[:, 128 * c : 128 * c + 128]
    return total


def kernel(
    n_sub, n_grp,
    loads_hbm, flex_hbm, schur_hbm, coupling_hbm, inverse_hbm, match_hbm, corner_hbm,
    out,
    loads, flex, schur, coupling, inverse, match, corner, corner_pad,
    halo, near_coupling, near_corner,
    perm, padded, wide_g, g_schur, g_schur_g, select, near_inverse, inv_hi, inv_lo,
    res, y_buf, free, z_buf, image,
    dense, recv1, part, chip, pair, recv2, total, rhs,
    local_sem, halo_send, halo_recv, near_send, near_recv,
    send1, rec1, send2, rec2, send3, rec3,
):
    s, g = lax.axis_index("sub"), lax.axis_index("grp")
    load_cases, interface = loads.shape
    face = interface // 4
    half = interface // 2
    size = inverse.shape[0]
    width = size // 2
    plain, wide = slice(0, width), slice(0, width + 128)
    corners = coupling.shape[0]
    row, column = s // SIDE, lax.rem(s, SIDE)
    rows_on = [lax.rem(row + d, SIDE) * SIDE for d in range(SIDE)]
    columns_on = [lax.rem(column + d, SIDE) for d in range(SIDE)]

    def sub_peer(k):
        return (rows_on[k // SIDE] + columns_on[k % SIDE], g)

    def z_peer(d):
        return (s, lax.rem(g + 2 * d, n_grp))

    other = (s, g + 1 - 2 * lax.rem(g, 2))
    near = (
        (lax.rem(s + n_sub - 1, n_sub), g), (lax.rem(s + 1, n_sub), g),
        (s, lax.rem(g + n_grp - 1, n_grp)), (s, lax.rem(g + 1, n_grp)),
    )

    def faces(f):
        return slice(face * f, face * f + face)

    def remote(src, dst, send, recv, to):
        pltpu.make_async_remote_copy(
            src_ref=src, dst_ref=dst, send_sem=send, recv_sem=recv, device_id=to, device_id_type=MESH
        ).start()

    def drain(ref, sem):
        pltpu.make_async_copy(ref, ref, sem).wait()

    sent = []

    def flush():
        for ref, sem in sent:
            drain(ref, sem)
        sent.clear()

    barrier = pltpu.get_barrier_semaphore()
    for d in range(1, n_sub):
        to = (lax.rem(s + d, n_sub), g)
        pl.semaphore_signal(barrier, inc=1, device_id=to, device_id_type=MESH)
    for d in RING:
        pl.semaphore_signal(barrier, inc=1, device_id=z_peer(d), device_id_type=MESH)
    for d in (1, n_grp - 1):
        to = (s, lax.rem(g + d, n_grp))
        pl.semaphore_signal(barrier, inc=1, device_id=to, device_id_type=MESH)

    sources = (
        (corner_hbm, corner), (coupling_hbm.at[0], coupling), (loads_hbm.at[0, 0], loads),
        (match_hbm.at[0, 0], match), (schur_hbm.at[0, 0], schur), (flex_hbm.at[0, 0], flex), (inverse_hbm, inverse),
    )
    local = []
    for i, (src, dst) in enumerate(sources):
        copy = pltpu.make_async_copy(src, dst, local_sem.at[i])
        copy.start()
        local.append(copy)
    corner_copy, coupling_copy, loads_copy, match_copy, schur_copy, flex_copy, inverse_copy = local

    corner_copy.wait()
    corner_pad[...] = jnp.full(corner_pad.shape, -1, jnp.int32)
    corner_pad[0:1, 0:corners] = corner[0]
    coupling_copy.wait()
    loads_copy.wait()
    pl.semaphore_wait(barrier, n_sub - 1 + len(RING) + 2)

    for f in range(4):
        o = OPPOSITE[f]
        remote(coupling.at[:, :, faces(f)], near_coupling.at[o], near_send.at[0], near_recv.at[0], near[f])
    for f in range(4):
        remote(corner_pad, near_corner.at[OPPOSITE[f]], near_send.at[1], near_recv.at[1], near[f])
    sent.append((near_coupling, near_send.at[0]))
    sent.append((near_corner, near_send.at[1]))

    def send_out(step, f0, ref):
        for f in (f0, f0 + 1):
            o = OPPOSITE[f]
            remote(ref.at[:, faces(f)], halo.at[step, o], halo_send.at[step, f0 // 2], halo_recv.at[step, f0 // 2], near[f])
        sent.append((halo.at[step, f0 : f0 + 2], halo_send.at[step, f0 // 2]))

    send_out(0, 0, loads)
    send_out(0, 2, loads)
    match_copy.wait()
    index = lax.broadcasted_iota(jnp.int32, (face, face), 0)
    for f in range(4):
        perm[f] = (index == match[f : f + 1, :]).astype(BF16)

    def neighbour(step, f):
        if f % 2 == 0:
            drain(halo.at[step, f : f + 2], halo_recv.at[step, f // 2])
        both = dot(stacked(halo[step, f]), perm[f])
        return both[:load_cases] + both[load_cases:]

    def add_g_schur(first, last):
        terms = jnp.concatenate([wide_g[first:last, :], wide_g[first + 128 : last + 128, :]], axis=0)
        for f in range(4):
            both = dot(terms, schur[:, faces(f)])
            hi, lo = split(0.5 * (both[: last - first] + both[last - first :]))
            g_schur[first:last, faces(f)] = hi
            g_schur[first + 128 : last + 128, faces(f)] = lo

    wide_g[...] = jnp.zeros(wide_g.shape, BF16)
    padded[...] = jnp.zeros(padded.shape, F32)
    for k in range(corners):
        padded[k : k + 1, :] = coupling[k]
    hi, lo = split(padded[...])
    wide_g[0:16, :] = hi
    wide_g[128:144, :] = lo
    g_schur[...] = jnp.zeros(g_schur.shape, BF16)
    schur_copy.wait()
    add_g_schur(0, 16)
    drain(near_coupling, near_recv.at[0])
    for f in range(4):
        for k in range(corners):
            padded[k : k + 1, faces(f)] = near_coupling[f, k]
        both = -dot(stacked(padded[:, faces(f)]), perm[f])
        start = 16 * f + 16
        wide_g[start : start + 16, faces(f)] = both[:16].astype(BF16)
        wide_g[start + 128 : start + 144, faces(f)] = both[16:].astype(BF16)
    drain(near_corner, near_recv.at[1])
    lane = lax.broadcasted_iota(jnp.int32, (8, 128), 1)
    numbers = jnp.where(lane < corners, corner_pad[...], -1)
    for f in range(4):
        start = 16 * f + 16
        inside = jnp.logical_and(lane >= start, lane < start + corners)
        numbers = jnp.where(inside, pltpu.roll(near_corner[f], start, 1), numbers)
    turned = jnp.broadcast_to(numbers.astype(F32)[0:1, :], (128, 128)).T
    unknown = lax.broadcasted_iota(jnp.int32, (128, size), 1).astype(F32)
    select[...] = (turned[:, 0:1] == unknown).astype(BF16)
    add_g_schur(16, 80)

    def start_coarse(it, mine):
        spread = dot(stacked(mine), select[...])
        spread = spread[:load_cases] + spread[load_cases:]
        for t in range(n_sub):
            lg, h = t % 8, t // 8
            dense[it, t] = spread[8 * lg : 8 * lg + 8, width * h : width * h + width]
        for k in FAR_FIRST:
            to = sub_peer(k)
            remote(dense.at[it, to[0]], recv1.at[it, k - 1], send1.at[it], rec1.at[it], to)
        sent.append((recv1.at[it], send1.at[it]))

    def middle_coarse(it, cut):
        drain(recv1.at[it], rec1.at[it])
        acc = dense[it, s]
        for k in range(1, n_sub):
            acc = acc + recv1[it, k - 1]
        part[it, :, :width] = acc
        remote(part.at[it, :, cut], chip.at[it, :, cut], send2.at[it, 0], rec2.at[it, 0], other)
        sent.append((chip.at[it, :, cut], send2.at[it, 0]))

    def third_coarse(it, cut):
        drain(chip.at[it, :, cut], rec2.at[it, 0])
        pair[it, :, cut] = part[it, :, cut] + chip[it, :, cut]
        for d in RING:
            remote(pair.at[it, :, cut], recv2.at[it, d - 1, :, cut], send2.at[it, 1], rec2.at[it, 1], z_peer(d))
        sent.append((recv2.at[it, :, :, cut], send2.at[it, 1]))

    def last_coarse(it, cut):
        drain(recv2.at[it, :, :, cut], rec2.at[it, 1])
        acc = pair[it, :, cut]
        for d in RING:
            acc = acc + recv2[it, d - 1, :, cut]
        total[it, :, cut] = acc
        rhs[it, s, :, cut] = acc
        for k in FAR_FIRST:
            remote(total.at[it, :, cut], rhs.at[it, s, :, cut], send3.at[it], rec3.at[it], sub_peer(k))
        sent.append((rhs.at[it, 0 : n_sub - 1, :, cut], send3.at[it]))

    def whole_coarse(it, cut):
        drain(rhs.at[it, 0 : n_sub - 1, :, cut], rec3.at[it])
        return stacked(
            jnp.concatenate(
                [
                    jnp.concatenate([rhs[it, 8 * h + lg, :, :width] for lg in range(8)], axis=0)
                    for h in range(2)
                ],
                axis=1,
            )
        )

    def pick(both):
        out = dot(both, near_inverse[...])
        return out[:load_cases, :128] + out[:load_cases, 128:] + out[load_cases:, :128]

    def lowered(both):
        low = dot(both, inv_hi[...])
        return low[:load_cases] + low[load_cases:] + dot(both[:load_cases], inv_lo[...])

    def twice(both, matrix, cut):
        out = dot(both, matrix[0:128, cut])
        return out[:load_cases] + out[load_cases:] + dot(both[:load_cases], matrix[128:256, cut])

    def row_of(a, b):
        return jnp.sum(jnp.concatenate([a, b], axis=0).T, axis=0, keepdims=True)

    def tile(a):
        return jnp.concatenate([a] * (face // 128), axis=1)

    def start_flex(it):
        for f in (2, 3):
            z_buf[it, :, faces(f)] = 0.5 * (y_buf[it, :, faces(f)] - neighbour(2 * it + 1, f))
        free[it] = dot(z_buf[it, :, half:].astype(BF16), flex[half:, :])

    def finish_flex(it):
        for f in (0, 1):
            z_buf[it, :, faces(f)] = 0.5 * (y_buf[it, :, faces(f)] - neighbour(2 * it + 1, f))
        direction = z_buf[it, :, :half].astype(BF16)
        for h in range(2):
            cut = slice(half * h, half * h + half)
            free[it, :, cut] = free[it, :, cut] + dot(direction, flex[:half, cut])
            send_out(2 * it + 2, 2 * h, free.at[it])

    for f in (2, 3):
        res[:, faces(f)] = loads[:, faces(f)] - neighbour(0, f)
    both = dot_nt((0.5 * res[:, half:]).astype(BF16), g_schur[:, half:])
    for f in (0, 1):
        res[:, faces(f)] = loads[:, faces(f)] - neighbour(0, f)
    weighted = (0.5 * res[...]).astype(BF16)
    both = both + dot_nt(weighted[:, :half], g_schur[:, :half])
    start_coarse(0, both[:, :128] + both[:, 128:])
    for h in range(2):
        cut = slice(half * h, half * h + half)
        y_buf[0, :, cut] = dot(weighted, schur[:, cut])
        send_out(1, 2 * h, y_buf.at[0])

    inverse_copy.wait()
    hi, lo = split(inverse[...].T)
    inv_hi[...] = hi
    inv_lo[...] = lo
    flex_copy.wait()

    middle_coarse(0, plain)
    start_flex(0)
    third_coarse(0, plain)
    finish_flex(0)
    rows = [row_of(lane_chunks(0.5 * res[...] * y_buf[0]), lane_chunks(z_buf[0] * free[0]))]

    both = dot_nt(wide_g[...], g_schur[...])
    hi, lo = split(0.5 * (both[:128, :128] + both[:128, 128:] + both[128:, :128]))
    g_schur_g[0:128, :] = hi
    g_schur_g[128:256, :] = lo
    flush()
    last_coarse(0, plain)
    for f in range(4):
        image[0, :, faces(f)] = free[0, :, faces(f)] - neighbour(2, f)
    weighted = (0.5 * image[0]).astype(BF16)
    y_buf[1] = dot(weighted, schur[...])
    both = dot_nt(weighted, g_schur[...])
    mine = both[:, :128] + both[:, 128:]
    chosen_hi = dot(select[...], inv_hi[...]).astype(BF16)
    chosen_lo = dot(select[...], inv_lo[...]).astype(BF16)
    both = dot_nt(inv_hi[...], jnp.concatenate([chosen_hi, chosen_lo], axis=0))
    hi, lo = split(both[:, :128] + both[:, 128:] + dot_nt(inv_lo[...], chosen_hi))
    near_inverse[:, 0:128] = hi
    near_inverse[:, 128:256] = lo
    both_rhs = whole_coarse(0, plain)
    both = stacked(pick(both_rhs))

    for h in range(2):
        cut = slice(half * h, half * h + half)
        y_buf[1, :, cut] = y_buf[1, :, cut] + twice(both, g_schur, cut)
        send_out(3, 2 * h, y_buf.at[1])
    start_coarse(1, mine + twice(both, g_schur_g, slice(0, 128)))
    for f in range(4):
        image[0, :, faces(f)] = image[0, :, faces(f)] + twice(both, wide_g, faces(f))
    low0 = lowered(both_rhs)
    rows.append(
        row_of(
            lane_chunks(0.5 * (image[0] * y_buf[0] + res[...] * y_buf[1])),
            lane_chunks(0.5 * image[0] * y_buf[1]),
        )
    )
    part[1, :, width:] = jnp.zeros((8, 128), F32)
    flush()
    start_flex(1)
    finish_flex(1)
    rows.append(row_of(lane_chunks(2.0 * z_buf[1] * free[0]), lane_chunks(z_buf[1] * free[1])))
    for i, r in enumerate(rows):
        part[1, i : i + 1, width:] = r
    middle_coarse(1, wide)
    third_coarse(1, wide)
    for f in range(4):
        image[1, :, faces(f)] = free[1, :, faces(f)] - neighbour(4, f)
    flush()
    last_coarse(1, wide)
    flush()
    both_rhs = whole_coarse(1, wide)
    both = stacked(pick(both_rhs))
    low1 = lowered(both_rhs)

    acc = rhs[1, 0, :, width:]
    for k in range(1, n_sub):
        acc = acc + rhs[1, k, :, width:]
    sums = []
    for i in range(len(rows)):
        turned = jnp.broadcast_to(acc[i : i + 1, :], (128, 128)).T
        sums += [turned[:load_cases], turned[load_cases:]]
    rz0, free_00, res_01, res_11, free_01, free_11 = sums
    a0 = rz0 / (free_00 + jnp.sum(low0 * low0, axis=1, keepdims=True))
    rz1 = rz0 - a0 * res_01 + a0 * a0 * res_11
    more = 1.0 + rz1 / rz0
    low = more[:, 0:1] * low0 - a0[:, 0:1] * low1
    curvature = (
        more * more * free_00 - more * a0 * free_01 + a0 * a0 * free_11 + jnp.sum(low * low, axis=1, keepdims=True)
    )
    a1 = rz1 / curvature
    first, second = a0 + a1 * more, a0 * a1
    for f in range(4):
        sign = 1.0 if f % 2 else -1.0
        one, two = tile(sign * first), tile(sign * second)
        out[:, f, :] = one * z_buf[0, :, faces(f)] - two * z_buf[1, :, faces(f)]
        out[:, f + 4, :] = (
            sign * res[:, faces(f)]
            - one * image[0, :, faces(f)]
            + two * (image[1, :, faces(f)] + twice(both, wide_g, faces(f)))
        )


def solution(mesh):
    n_sub, n_grp = mesh.shape["sub"], mesh.shape["grp"]

    def shards(loads, flex, schur, coupling, inverse, match, corner):
        load_cases, interface = loads.shape[2:]
        face = interface // 4
        corners, size = coupling.shape[2], inverse.shape[0]
        vmem, dma = pltpu.VMEM, pltpu.SemaphoreType.DMA
        flat = (load_cases, interface)
        block, wide = (8, size // 2), (8, size // 2 + 128)
        scratch = [
            vmem(flat, F32), vmem((interface, interface), BF16), vmem((interface, interface), BF16),
            vmem((corners, 1, interface), F32), vmem((size, size), F32), vmem((4, face), jnp.int32),
            vmem(corner.shape, jnp.int32), vmem((8, 128), jnp.int32),
            vmem((5, 4, load_cases, face), F32), vmem((4, corners, 1, face), F32), vmem((4, 8, 128), jnp.int32),
            vmem((4, face, face), BF16), vmem((16, interface), F32), vmem((256, interface), BF16),
            vmem((256, interface), BF16), vmem((256, 128), BF16), vmem((128, size), BF16),
            vmem((size, 256), BF16), vmem((size, size), BF16), vmem((size, size), BF16),
            vmem(flat, F32), vmem((2,) + flat, F32), vmem((2,) + flat, F32), vmem((2,) + flat, F32),
            vmem((2,) + flat, F32),
            vmem((2, n_sub) + block, F32), vmem((2, n_sub - 1) + block, F32), vmem((2,) + wide, F32),
            vmem((2,) + wide, F32), vmem((2,) + wide, F32), vmem((2, len(RING)) + wide, F32), vmem((2,) + wide, F32),
            vmem((2, n_sub) + wide, F32),
            dma((7,)), dma((5, 2)), dma((5, 2)), dma((2,)), dma((2,)),
            dma((2,)), dma((2,)), dma((2, 2)), dma((2, 2)), dma((2,)), dma((2,)),
        ]
        out = pl.pallas_call(
            functools.partial(kernel, n_sub, n_grp),
            out_shape=jax.ShapeDtypeStruct((load_cases, 8, face), F32),
            in_specs=[HBM] * 7,
            out_specs=VMEM,
            scratch_shapes=scratch,
            compiler_params=pltpu.CompilerParams(
                collective_id=0, has_side_effects=True, vmem_limit_bytes=48 * 2**20
            ),
            name="cg",
        )(
            *(
                pltpu.with_memory_space_constraint(x, pltpu.HBM)
                for x in (loads, flex, schur, coupling.transpose(0, 2, 1, 3), inverse, match, corner)
            )
        )
        out = out[None, None]
        return out[:, :, :, :4], out[:, :, :, 4:]

    split4 = P("sub", "grp", None, None)
    return jax.shard_map(
        shards,
        mesh=mesh,
        in_specs=(split4, split4, split4, split4, P(), split4, P("sub", "grp", None)),
        out_specs=(P("sub", "grp", None, None, None), P("sub", "grp", None, None, None)),
        check_vma=False,
    )
```
